32 devices in a mesh: groups: 2 (over x), elec: 16 (over z, y, core).
Axes of the slice: x: 2, y: 2, z: 4, core: 2. Of those that a mesh axis runs over, the one named last changes fastest.
Arguments:
- features: bfloat16 [131072, 256], P(('groups', 'elec')), parts along dimension 0, may hold values from -6 to 6
- assignment: int32 [131072], P(('groups', 'elec')), parts along dimension 0, may hold values from 0 to 65535, as said below
- pairs: int32 [2048, 3], P(('groups', 'elec')), parts along dimension 0, may hold values from 0 to 1023, as said below
- w_query: bfloat16 [256, 256], replicated
- w_key: bfloat16 [256, 256], replicated
- w_value: bfloat16 [256, 256], replicated, may hold values from -0.375 to 0.375
- w_out: bfloat16 [256, 256], replicated, may hold values from -0.375 to 0.375
- w_mix: bfloat16 [256, 256], replicated, may hold values from -0.375 to 0.375
Outputs:
- mixed: bfloat16 [131072, 256], P(('groups', 'elec')), parts along dimension 0
The draws below stay inside these ranges and needn't reach their ends.
There are 2 independent parts, one for each index of `groups`. The reference program is written for one: setup_inputs(seed, part) draws one part's arguments, and reference() takes and returns one part's arrays. A program takes and returns all parts, laid end to end along the dimension named above; an argument that names none is the same for every part. Nothing has to cross between parts.
Inputs may be any that keep to these rules, and one draw needn't show every extreme that they name: assignment is a permutation of the rows; each group of 512 rows of one walker on one device is filled from electrons of that same group. pairs[b, :] name blocks of block b's own walker (its blocks lie on the 8 devices whose index has the same remainder modulo 1024 // 512 as block b's device, 8 on each). Over the 64 reader blocks of one device, at most 25 of the listed key blocks lie on any one device (blocks d * 64 to (d + 1) * 64 - 1 lie on device d), and exactly 25 on some device.
All inputs are finite; a program needn't handle non-finite values.
Results may differ from the reference program's by a relative error of at most 0.0078.
Values may be sent and summed in bfloat16 or wider, within the bound.
A program may use at most 128 MiB of HBM per device.

```python
import jax
import jax.numpy as jnp
from jax import lax

D = 256
HEADS = 16
HEAD_DIM = 16
CLUSTER = 64
PAIRS = 3
SPAN = 8
SUB = 8
BLK_DEV = 64
BLOCKS = 1024
ROWS = 65536
CAP = 25


def draw_assignment(key, part):
    group_count = ROWS // (SUB * CLUSTER)
    rows_each = SUB * CLUSTER
    orders = jax.vmap(lambda k: jax.random.permutation(k, rows_each))(jax.random.split(key, group_count))
    offsets = jnp.arange(group_count, dtype=jnp.int32)[:, None] * rows_each
    return (orders.astype(jnp.int32) + offsets).reshape(-1).astype(jnp.int32)


def draw_pairs(key, part):
    shard_count = BLOCKS // BLK_DEV
    stride = shard_count // SPAN
    wanted = BLK_DEV * PAIRS
    rest_count = wanted - SPAN
    rest_cap = CAP - 1
    rest_slots = SPAN * rest_cap

    def one_device(k, device):
        k_perm, k_full, k_shuffle, k_local, k_owner = jax.random.split(k, 5)
        position = device // stride
        group_first = device % stride
        first_owner = jax.random.permutation(k_owner, SPAN).astype(jnp.int32)
        offset = (position - first_owner) % SPAN
        lowbit = jnp.where(offset == 0, SPAN, offset & -offset)
        first_within = (position // lowbit % 2).astype(jnp.int32)
        order_scores = jax.random.permutation(k_perm, rest_slots).astype(jnp.int32)
        full_owner = jax.random.randint(k_full, (), 0, SPAN)
        slot_ids = jnp.arange(rest_slots, dtype=jnp.int32)
        ranked = order_scores - jnp.where(slot_ids // rest_cap == full_owner, rest_slots, 0)
        order = jnp.argsort(ranked, stable=True)
        chosen = order[:rest_count]
        shuffle = jax.random.permutation(k_shuffle, rest_count)
        rest_owner = (chosen[shuffle] // rest_cap).astype(jnp.int32)
        rest_within = jax.random.randint(k_local, (rest_count,), 0, SUB).astype(jnp.int32)
        owner_pos = jnp.concatenate([first_owner, rest_owner])
        within = jnp.concatenate([first_within, rest_within])
        entry = jnp.arange(wanted, dtype=jnp.int32)
        walker_slot = entry // PAIRS // SUB
        listed = (group_first + owner_pos * stride) * BLK_DEV + walker_slot * SUB + within
        return listed.reshape(BLK_DEV, PAIRS)
    devices = jnp.arange(shard_count, dtype=jnp.int32)
    result = jax.vmap(one_device)(jax.random.split(key, shard_count), devices)
    return result.reshape(BLOCKS, PAIRS).astype(jnp.int32)


def projection_pair(key):
    k_one, k_two = jax.random.split(jax.random.fold_in(key, 7), 2)
    first = jax.random.normal(k_one, (D, D), jnp.float32) / D ** 0.5
    second = jax.random.normal(k_two, (D, D), jnp.float32) / D ** 0.5
    return (first, second)


def draw_w_query(key, part):
    return projection_pair(key)[0].astype(jnp.bfloat16)


def draw_w_key(key, part):
    return projection_pair(key)[1].astype(jnp.bfloat16)


def levels(own_key, dims, shards, least, top_value):
    level = 1.0
    for dim, parts in shards:
        draws = jax.random.uniform(jax.random.fold_in(jax.random.fold_in(own_key, 6), dim), (parts,), jnp.float32, least / len(shards), top_value / len(shards))
        level = level * jnp.repeat(jnp.exp(draws), dims[dim] // parts).reshape((-1,) + (1,) * (len(dims) - 1 - dim))
    return level


def noise(stream_key, shape, spread, bound, pieces=(), held_as=jnp.bfloat16):
    values = spread * jax.random.normal(stream_key, shape, jnp.float32)
    if pieces:
        values = values * levels(stream_key, shape, pieces, -0.22, 0.18)
    return jnp.clip(values, -bound, bound).astype(held_as)


def setup_inputs(seed: int = 0, part: int = 0) -> dict:
    streams_of = jax.random.split(jax.random.key(seed), 9)
    part_splits = jax.random.split(jax.random.fold_in(streams_of[8], part), 9)
    return {
        "features": noise(part_splits[0], (ROWS, D), 1.0, 6.0, ((0, 16),)),
        "assignment": draw_assignment(jax.random.fold_in(jax.random.fold_in(streams_of[8], part), 71), part),
        "pairs": draw_pairs(jax.random.fold_in(jax.random.fold_in(streams_of[8], part), 71), part),
        "w_query": draw_w_query(jax.random.fold_in(streams_of[8], 71), part),
        "w_key": draw_w_key(jax.random.fold_in(streams_of[8], 71), part),
        "w_value": noise(streams_of[5], (D, D), D ** -0.5, 0.375),
        "w_out": noise(streams_of[6], (D, D), D ** -0.5, 0.375),
        "w_mix": noise(streams_of[7], (D, D), D ** -0.5, 0.375),
    }


def layer_norm(rows):
    mean = lax.optimization_barrier(jnp.mean(rows, axis=-1, keepdims=True))
    centred = rows - mean
    variance = lax.optimization_barrier(jnp.mean(centred * centred, axis=-1, keepdims=True))
    return centred * lax.rsqrt(variance + 1e-05)

def reference(features, assignment, pairs, w_query, w_key, w_value, w_out, w_mix):
    placed = jnp.take(features, assignment, axis=0)
    normed = layer_norm(placed.astype(jnp.float32)).astype(jnp.bfloat16)
    query = jnp.dot(normed, w_query, preferred_element_type=jnp.float32).astype(jnp.bfloat16)
    keys = jnp.dot(normed, w_key, preferred_element_type=jnp.float32).astype(jnp.bfloat16)
    values = jnp.dot(normed, w_value, preferred_element_type=jnp.float32).astype(jnp.bfloat16)
    query_blocks = query.reshape(BLOCKS, CLUSTER, D)
    key_blocks = keys.reshape(BLOCKS, CLUSTER, D)
    value_blocks = values.reshape(BLOCKS, CLUSTER, D)
    scale = 1.0 / HEAD_DIM ** 0.5

    def attend(args):
        block_query, block_index, listed = args
        chosen = jnp.concatenate([block_index[None], listed]).astype(jnp.int32)
        set_keys = jnp.take(key_blocks, chosen, axis=0).reshape(-1, HEADS, HEAD_DIM).astype(jnp.float32)
        set_values = jnp.take(value_blocks, chosen, axis=0).reshape(-1, HEADS, HEAD_DIM).astype(jnp.float32)
        heads_query = block_query.reshape(CLUSTER, HEADS, HEAD_DIM).astype(jnp.float32)
        scores = jnp.einsum('qhd,khd->hqk', heads_query, set_keys) * scale
        weights = jax.nn.softmax(scores, axis=-1).astype(jnp.bfloat16)
        result = jnp.einsum('hqk,khd->qhd', weights.astype(jnp.float32), set_values)
        return result.astype(jnp.bfloat16).reshape(CLUSTER, D)
    attended = lax.map(attend, (query_blocks, jnp.arange(BLOCKS, dtype=jnp.int32), pairs), batch_size=64)
    attended = attended.reshape(ROWS, D)
    middle = (placed.astype(jnp.float32) + jnp.dot(attended, w_out, preferred_element_type=jnp.float32)).astype(jnp.bfloat16)
    second = layer_norm(middle.astype(jnp.float32)).astype(jnp.bfloat16)
    mixed = middle.astype(jnp.float32) + jnp.tanh(jnp.dot(second, w_mix, preferred_element_type=jnp.float32))
    return mixed.astype(jnp.bfloat16)
```

```python
import functools
import math

import jax
import jax.numpy as jnp
from jax import lax
from jax.experimental import pallas as pl
from jax.experimental.pallas import tpu as pltpu
from jax.sharding import PartitionSpec as P

HEADS = 16
SPAN = 8
COPIES = 4
LANES = 128
MESH = pl.DeviceIdType.MESH


def layer_norm(rows):
    mean = jnp.mean(rows, axis=-1, keepdims=True)
    centred = rows - mean
    variance = jnp.mean(centred * centred, axis=-1, keepdims=True)
    return centred * lax.rsqrt(variance + 1e-05)


def slot_table(listed, block_count, capacity, position, stride):
    flattened = listed.reshape(-1)
    owner_device = flattened // block_count
    within = flattened % block_count
    entries = flattened.shape[0]
    offset = (position - owner_device // stride) % SPAN
    alike = offset[:, None] == offset[None, :]
    earlier = jnp.arange(entries)[None, :] < jnp.arange(entries)[:, None]
    ranking = jnp.sum(jnp.where(alike & earlier, 1, 0), axis=1).astype(jnp.int32)
    slots = offset * capacity + ranking
    columns = jnp.arange(SPAN * LANES, dtype=jnp.int32)
    matches = (offset * LANES + ranking)[None, :] == columns[:, None]
    tables = jnp.sum(jnp.where(matches, within[None, :], 0), axis=1)
    return slots, tables.astype(jnp.int32).reshape(SPAN, 1, LANES)


def place_kernel(local_ref, features_ref, placed_ref, normed_ref):
    size = features_ref.shape[0]
    one_hot = jnp.where(
        lax.broadcasted_iota(jnp.int32, (size, size), 0) == local_ref[0], 1.0, 0.0
    ).astype(jnp.bfloat16)
    placed = lax.dot_general(
        one_hot, features_ref[...], (((0,), (0,)), ((), ())), preferred_element_type=jnp.float32
    )
    placed_ref[...] = placed.astype(jnp.bfloat16)
    normed_ref[...] = layer_norm(placed).astype(jnp.bfloat16)


def exchange_kernel(
    capacity, stride, blocks_ref, tables_ref, arrived_ref,
    wanted, wanted_s, outbox, t_send, t_recv, d_send, d_recv, local_sem,
):
    me = lax.axis_index("elec")
    group = lax.axis_index("groups")
    peers = lax.axis_size("elec")
    cluster = blocks_ref.shape[1]

    def toward(step):
        return (group, lax.rem(me + step * stride + peers, peers))

    barrier = pltpu.get_barrier_semaphore()
    for step in range(1, SPAN):
        pl.semaphore_signal(barrier, inc=1, device_id=toward(step), device_id_type=MESH)
    pl.semaphore_wait(barrier, SPAN - 1)

    order = sorted(range(1, SPAN), key=lambda s: abs(s - SPAN // 2))
    asks = {}
    for step in order:
        asks[step] = pltpu.make_async_remote_copy(
            src_ref=tables_ref.at[step], dst_ref=wanted.at[step],
            send_sem=t_send.at[step], recv_sem=t_recv.at[step],
            device_id=toward(-step), device_id_type=MESH,
        )
        asks[step].start()

    def gather(step, source):
        copy = pltpu.make_async_copy(source, wanted_s.at[step], local_sem.at[step])
        copy.start()
        copy.wait()

        def one(k, carry):
            start = pl.multiple_of(k * cluster, cluster)
            outbox[step, pl.ds(start, cluster), :] = blocks_ref[wanted_s[step, 0, k]]
            return carry

        lax.fori_loop(0, capacity, one, 0)

    sends = []
    for step in order:
        asks[step].wait_recv()
        gather(step, wanted.at[step])
        send = pltpu.make_async_remote_copy(
            src_ref=outbox.at[step], dst_ref=arrived_ref.at[step],
            send_sem=d_send.at[step], recv_sem=d_recv.at[step],
            device_id=toward(step), device_id_type=MESH,
        )
        send.start()
        sends.append(send)
    gather(0, tables_ref.at[0])
    own = pltpu.make_async_copy(outbox.at[0], arrived_ref.at[0], local_sem.at[SPAN])
    own.start()
    for step in order:
        asks[step].wait_send()
    own.wait()
    for send in sends:
        send.wait()


def attend_kernel(
    slots_ref, placed_ref, normed_ref, arrived_ref, wqt_ref, wk_ref, wvt_ref, wo_ref, wm_ref,
    out_ref, projected,
):
    cluster, width = arrived_ref.shape[1:]
    rows = placed_ref.shape[0]
    blocks = rows // cluster
    pair_count = slots_ref.shape[0] // (blocks * pl.num_programs(0))
    head_width = width // HEADS
    wide = COPIES * cluster
    part = COPIES * head_width
    first = pl.program_id(0) * blocks
    f32, bf16 = jnp.float32, jnp.bfloat16
    row = lax.broadcasted_iota(jnp.int32, (width, wide), 0)
    column = lax.broadcasted_iota(jnp.int32, (width, wide), 1)
    same = (row // head_width) % COPIES == column // cluster
    scale = math.log2(math.e) / head_width**0.5
    keep = jnp.where(same, scale, 0.0).astype(f32)
    nt = (((1,), (1,)), ((), ()))

    def one(j, carry):
        start = pl.multiple_of(j * cluster, cluster)
        own = normed_ref[pl.ds(start, cluster), :]
        base = (first + j) * pair_count
        listed = [arrived_ref[slots_ref[base + p]] for p in range(pair_count)]
        key_rows = jnp.concatenate([own] + listed, axis=0)
        query = lax.dot_general(
            wqt_ref[...], jnp.concatenate([own] * COPIES, axis=0), nt, preferred_element_type=f32
        )
        query = (query * keep).astype(bf16)
        keys = jnp.dot(key_rows, wk_ref[...], preferred_element_type=f32).astype(bf16)
        values = lax.dot_general(wvt_ref[...], key_rows, nt, preferred_element_type=f32).astype(bf16)
        pieces = []
        blank = jnp.zeros((part, wide), bf16)
        for g in range(HEADS // COPIES):
            band = g * part // LANES * LANES
            mine = query[g * part : (g + 1) * part, :]
            halves = [blank] * (LANES // part)
            halves[(g * part - band) // part] = mine
            scores = jnp.dot(
                keys[:, band : band + LANES], jnp.concatenate(halves, axis=0),
                preferred_element_type=f32,
            )
            top = jnp.max(scores, axis=0, keepdims=True)
            weights = jnp.exp2(scores - top)
            total = jnp.sum(weights, axis=0, keepdims=True)
            result = jnp.dot(
                values[g * part : (g + 1) * part, :], weights.astype(bf16),
                preferred_element_type=f32,
            )
            pieces.append(result * (1.0 / total))
        attended = jnp.where(same, jnp.concatenate(pieces, axis=0), 0.0).astype(bf16)
        spread = jnp.dot(attended.T, wo_ref[...], preferred_element_type=f32)
        total = spread[:cluster]
        for c in range(1, COPIES):
            total = total + spread[c * cluster : (c + 1) * cluster]
        projected[pl.ds(start, cluster), :] = total
        return carry

    lax.fori_loop(0, blocks, one, 0, unroll=2)
    middle = (placed_ref[...].astype(f32) + projected[...]).astype(bf16)
    middle = middle.astype(f32)
    second = layer_norm(middle).astype(bf16)
    mixed = middle + jnp.tanh(jnp.dot(second, wm_ref[...], preferred_element_type=f32))
    out_ref[...] = mixed.astype(bf16)


def body(features, assignment, pairs, w_query, w_key, w_value, w_out, w_mix):
    rows_dev, width = features.shape
    block_count, pair_count = pairs.shape
    cluster = rows_dev // block_count
    capacity = (block_count * pair_count + SPAN - 1) // SPAN + 1
    stride = lax.axis_size("elec") // SPAN
    device_index = lax.axis_index("elec")
    position = device_index // stride
    group_rows = SPAN * cluster
    groups = rows_dev // group_rows
    bf16 = jnp.bfloat16

    local = (assignment - device_index * rows_dev).reshape(groups, 1, group_rows)
    local = local - group_rows * jnp.arange(groups, dtype=jnp.int32)[:, None, None]
    tile = pl.BlockSpec((group_rows, width), lambda i: (i, 0))
    placed, normed = pl.pallas_call(
        place_kernel,
        grid=(groups,),
        in_specs=[pl.BlockSpec((1, 1, group_rows), lambda i: (i, 0, 0)), tile],
        out_specs=[tile, tile],
        out_shape=[jax.ShapeDtypeStruct((rows_dev, width), bf16)] * 2,
    )(local, features)

    slots, tables = slot_table(pairs, block_count, capacity, position, stride)
    arrived = pl.pallas_call(
        functools.partial(exchange_kernel, capacity, stride),
        in_specs=[pl.BlockSpec(memory_space=pltpu.VMEM)] * 2,
        out_specs=pl.BlockSpec(memory_space=pl.ANY),
        out_shape=jax.ShapeDtypeStruct((SPAN, capacity * cluster, width), bf16),
        scratch_shapes=[
            pltpu.VMEM((SPAN, 1, LANES), jnp.int32),
            pltpu.SMEM((SPAN, 1, LANES), jnp.int32),
            pltpu.VMEM((SPAN, capacity * cluster, width), bf16),
            pltpu.SemaphoreType.DMA((SPAN,)),
            pltpu.SemaphoreType.DMA((SPAN,)),
            pltpu.SemaphoreType.DMA((SPAN,)),
            pltpu.SemaphoreType.DMA((SPAN,)),
            pltpu.SemaphoreType.DMA((SPAN + 1,)),
        ],
        compiler_params=pltpu.CompilerParams(
            collective_id=0, has_side_effects=True, vmem_limit_bytes=32 * 2**20
        ),
    )(normed.reshape(block_count, cluster, width), tables)
    arrived = arrived.reshape(SPAN * capacity, cluster, width)

    tile = pl.BlockSpec((group_rows, width), lambda i, s: (i, 0))
    weight = pl.BlockSpec((width, width), lambda i, s: (0, 0))
    return pl.pallas_call(
        attend_kernel,
        grid_spec=pltpu.PrefetchScalarGridSpec(
            num_scalar_prefetch=1,
            grid=(groups,),
            in_specs=[
                tile,
                tile,
                pl.BlockSpec(arrived.shape, lambda i, s: (0, 0, 0)),
            ]
            + [weight] * 5,
            out_specs=tile,
            scratch_shapes=[pltpu.VMEM((group_rows, width), jnp.float32)],
        ),
        out_shape=jax.ShapeDtypeStruct((rows_dev, width), bf16),
        compiler_params=pltpu.CompilerParams(vmem_limit_bytes=48 * 2**20),
    )(slots, placed, normed, arrived, w_query.T, w_key, w_value.T, w_out, w_mix)


def solution(mesh):
    placed = (
        P(("groups", "elec"), None),
        P(("groups", "elec")),
        P(("groups", "elec"), None),
        P(),
        P(),
        P(),
        P(),
        P(),
    )
    return jax.shard_map(
        body, mesh=mesh, in_specs=placed, out_specs=P(("groups", "elec"), None), check_vma=False
    )
```

```python
import functools
import math

import jax
import jax.numpy as jnp
from jax import lax
from jax.experimental import pallas as pl
from jax.experimental.pallas import tpu as pltpu
from jax.sharding import PartitionSpec as P

HEADS = 16
SPAN = 8
LANES = 128
MESH = pl.DeviceIdType.MESH


def layer_norm(rows):
    mean = jnp.mean(rows, axis=-1, keepdims=True)
    centred = rows - mean
    variance = jnp.mean(centred * centred, axis=-1, keepdims=True)
    return centred * lax.rsqrt(variance + 1e-05)


def slot_table(listed, block_count, capacity, position, stride):
    flattened = listed.reshape(-1)
    owner_device = flattened // block_count
    within = flattened % block_count
    entries = flattened.shape[0]
    offset = (position - owner_device // stride) % SPAN
    alike = offset[:, None] == offset[None, :]
    earlier = jnp.arange(entries)[None, :] < jnp.arange(entries)[:, None]
    ranking = jnp.sum(jnp.where(alike & earlier, 1, 0), axis=1).astype(jnp.int32)
    slots = offset * capacity + ranking
    columns = jnp.arange(SPAN * LANES, dtype=jnp.int32)
    matches = (offset * LANES + ranking)[None, :] == columns[:, None]
    tables = jnp.sum(jnp.where(matches, within[None, :], 0), axis=1)
    return slots, tables.astype(jnp.int32).reshape(SPAN, 1, LANES)


def place_kernel(local_ref, features_ref, placed_ref, normed_ref):
    size = features_ref.shape[0]
    one_hot = jnp.where(
        lax.broadcasted_iota(jnp.int32, (size, size), 0) == local_ref[0], 1.0, 0.0
    ).astype(jnp.bfloat16)
    placed = lax.dot_general(
        one_hot, features_ref[...], (((0,), (0,)), ((), ())), preferred_element_type=jnp.float32
    )
    placed_ref[...] = placed.astype(jnp.bfloat16)
    normed_ref[...] = layer_norm(placed).astype(jnp.bfloat16)


def exchange_kernel(
    capacity, stride, blocks_ref, tables_ref, arrived_ref,
    wanted, wanted_s, outbox, t_send, t_recv, d_send, d_recv, local_sem,
):
    me = lax.axis_index("elec")
    group = lax.axis_index("groups")
    peers = lax.axis_size("elec")
    cluster = blocks_ref.shape[1]

    def toward(step):
        return (group, lax.rem(me + step * stride + peers, peers))

    barrier = pltpu.get_barrier_semaphore()
    for step in range(1, SPAN):
        pl.semaphore_signal(barrier, inc=1, device_id=toward(step), device_id_type=MESH)
    pl.semaphore_wait(barrier, SPAN - 1)

    order = sorted(range(1, SPAN), key=lambda s: abs(s - SPAN // 2))
    asks = {}
    for step in order:
        asks[step] = pltpu.make_async_remote_copy(
            src_ref=tables_ref.at[step], dst_ref=wanted.at[step],
            send_sem=t_send.at[step], recv_sem=t_recv.at[step],
            device_id=toward(-step), device_id_type=MESH,
        )
        asks[step].start()

    def gather(step, source):
        copy = pltpu.make_async_copy(source, wanted_s.at[step], local_sem.at[step])
        copy.start()
        copy.wait()

        def one(k, carry):
            start = pl.multiple_of(k * cluster, cluster)
            outbox[step, pl.ds(start, cluster), :] = blocks_ref[wanted_s[step, 0, k]]
            return carry

        lax.fori_loop(0, capacity, one, 0)

    sends = []
    for step in order:
        asks[step].wait_recv()
        gather(step, wanted.at[step])
        send = pltpu.make_async_remote_copy(
            src_ref=outbox.at[step], dst_ref=arrived_ref.at[step],
            send_sem=d_send.at[step], recv_sem=d_recv.at[step],
            device_id=toward(step), device_id_type=MESH,
        )
        send.start()
        sends.append(send)
    gather(0, tables_ref.at[0])
    own = pltpu.make_async_copy(outbox.at[0], arrived_ref.at[0], local_sem.at[SPAN])
    own.start()
    for step in order:
        asks[step].wait_send()
    own.wait()
    for send in sends:
        send.wait()


def attend_kernel(
    slots_ref, placed_ref, normed_ref, arrived_ref, wq_ref, wk_ref, wv_ref, wo_ref, wm_ref,
    out_ref, queries, attended,
):
    cluster, width = arrived_ref.shape[1:]
    rows = placed_ref.shape[0]
    blocks = rows // cluster
    pair_count = slots_ref.shape[0] // (blocks * pl.num_programs(0))
    head_width = width // HEADS
    half = LANES // 2
    per = half // head_width
    first = pl.program_id(0) * blocks
    f32, bf16 = jnp.float32, jnp.bfloat16
    lane = lax.broadcasted_iota(jnp.int32, (cluster, LANES), 1)
    low = lane < half
    low_keys = lax.broadcasted_iota(jnp.int32, ((pair_count + 1) * cluster, LANES), 1) < half
    chosen = [jnp.where(lane // head_width == c, 1.0, 0.0).astype(bf16) for c in range(2 * per)]
    own_head = lane % half // head_width
    scale = math.log2(math.e) / head_width**0.5
    queries[...] = (
        jnp.dot(normed_ref[...], wq_ref[...], preferred_element_type=f32) * scale
    ).astype(bf16)

    def one(j, carry):
        start = pl.multiple_of(j * cluster, cluster)
        base = (first + j) * pair_count
        listed = [arrived_ref[slots_ref[base + p]] for p in range(pair_count)]
        key_rows = jnp.concatenate([normed_ref[pl.ds(start, cluster), :]] + listed, axis=0)
        keys = jnp.dot(key_rows, wk_ref[...], preferred_element_type=f32).astype(bf16)
        values = jnp.dot(key_rows, wv_ref[...], preferred_element_type=f32)
        for band in range(0, width, LANES):
            query = queries[pl.ds(start, cluster), band : band + LANES]
            band_keys = keys[:, band : band + LANES]
            band_values = values[:, band : band + LANES]
            folded = []
            for side in range(2):
                stacked = jnp.concatenate(
                    [query * chosen[side * per + c] for c in range(per)], axis=0
                )
                scores = lax.dot_general(
                    stacked, band_keys, (((1,), (1,)), ((), ())), preferred_element_type=f32
                )
                weights = jnp.exp2(scores - jnp.max(scores, axis=1, keepdims=True)).astype(bf16)
                with_ones = (
                    jnp.where(low_keys, band_values, 1.0)
                    if side == 0
                    else jnp.where(low_keys, 1.0, band_values)
                ).astype(bf16)
                result = jnp.dot(weights, with_ones, preferred_element_type=f32)
                kept = result[(per - 1) * cluster :]
                for c in range(per - 1):
                    kept = jnp.where(own_head == c, result[c * cluster : (c + 1) * cluster], kept)
                folded.append(kept)
            numerator = jnp.where(low, folded[0], folded[1])
            denominator = pltpu.roll(jnp.where(low, folded[1], folded[0]), half, 1)
            attended[pl.ds(start, cluster), band : band + LANES] = (
                numerator / denominator
            ).astype(bf16)
        return carry

    lax.fori_loop(0, blocks, one, 0, unroll=True)
    projected = jnp.dot(attended[...], wo_ref[...], preferred_element_type=f32)
    middle = (placed_ref[...].astype(f32) + projected).astype(bf16).astype(f32)
    second = layer_norm(middle).astype(bf16)
    mixed = middle + jnp.tanh(jnp.dot(second, wm_ref[...], preferred_element_type=f32))
    out_ref[...] = mixed.astype(bf16)


def body(features, assignment, pairs, w_query, w_key, w_value, w_out, w_mix):
    rows_dev, width = features.shape
    block_count, pair_count = pairs.shape
    cluster = rows_dev // block_count
    capacity = (block_count * pair_count + SPAN - 1) // SPAN + 1
    stride = lax.axis_size("elec") // SPAN
    device_index = lax.axis_index("elec")
    position = device_index // stride
    group_rows = SPAN * cluster
    groups = rows_dev // group_rows
    bf16 = jnp.bfloat16

    local = (assignment - device_index * rows_dev).reshape(groups, 1, group_rows)
    local = local - group_rows * jnp.arange(groups, dtype=jnp.int32)[:, None, None]
    tile = pl.BlockSpec((group_rows, width), lambda i: (i, 0))
    placed, normed = pl.pallas_call(
        place_kernel,
        grid=(groups,),
        in_specs=[pl.BlockSpec((1, 1, group_rows), lambda i: (i, 0, 0)), tile],
        out_specs=[tile, tile],
        out_shape=[jax.ShapeDtypeStruct((rows_dev, width), bf16)] * 2,
    )(local, features)

    slots, tables = slot_table(pairs, block_count, capacity, position, stride)
    arrived = pl.pallas_call(
        functools.partial(exchange_kernel, capacity, stride),
        in_specs=[pl.BlockSpec(memory_space=pltpu.VMEM)] * 2,
        out_specs=pl.BlockSpec(memory_space=pl.ANY),
        out_shape=jax.ShapeDtypeStruct((SPAN, capacity * cluster, width), bf16),
        scratch_shapes=[
            pltpu.VMEM((SPAN, 1, LANES), jnp.int32),
            pltpu.SMEM((SPAN, 1, LANES), jnp.int32),
            pltpu.VMEM((SPAN, capacity * cluster, width), bf16),
            pltpu.SemaphoreType.DMA((SPAN,)),
            pltpu.SemaphoreType.DMA((SPAN,)),
            pltpu.SemaphoreType.DMA((SPAN,)),
            pltpu.SemaphoreType.DMA((SPAN,)),
            pltpu.SemaphoreType.DMA((SPAN + 1,)),
        ],
        compiler_params=pltpu.CompilerParams(
            collective_id=0, has_side_effects=True, vmem_limit_bytes=32 * 2**20
        ),
    )(normed.reshape(block_count, cluster, width), tables)
    arrived = arrived.reshape(SPAN * capacity, cluster, width)

    tile = pl.BlockSpec((group_rows, width), lambda i, s: (i, 0))
    weight = pl.BlockSpec((width, width), lambda i, s: (0, 0))
    return pl.pallas_call(
        attend_kernel,
        grid_spec=pltpu.PrefetchScalarGridSpec(
            num_scalar_prefetch=1,
            grid=(groups,),
            in_specs=[
                tile,
                tile,
                pl.BlockSpec(arrived.shape, lambda i, s: (0, 0, 0)),
            ]
            + [weight] * 5,
            out_specs=tile,
            scratch_shapes=[pltpu.VMEM((group_rows, width), bf16)] * 2,
        ),
        out_shape=jax.ShapeDtypeStruct((rows_dev, width), bf16),
        compiler_params=pltpu.CompilerParams(vmem_limit_bytes=48 * 2**20),
    )(slots, placed, normed, arrived, w_query, w_key, w_value, w_out, w_mix)


def solution(mesh):
    placed = (
        P(("groups", "elec"), None),
        P(("groups", "elec")),
        P(("groups", "elec"), None),
        P(),
        P(),
        P(),
        P(),
        P(),
    )
    return jax.shard_map(
        body, mesh=mesh, in_specs=placed, out_specs=P(("groups", "elec"), None), check_vma=False
    )
```

```python
import functools
import math

import jax
import jax.numpy as jnp
from jax import lax
from jax.experimental import pallas as pl
from jax.experimental.pallas import tpu as pltpu
from jax.sharding import PartitionSpec as P

HEADS = 16
SPAN = 8
LANES = 128
MESH = pl.DeviceIdType.MESH


def layer_norm(rows):
    mean = jnp.mean(rows, axis=-1, keepdims=True)
    centred = rows - mean
    variance = jnp.mean(centred * centred, axis=-1, keepdims=True)
    return centred * lax.rsqrt(variance + 1e-05)


def slot_table(listed, block_count, capacity, position, stride):
    flattened = listed.reshape(-1)
    owner_device = flattened // block_count
    within = flattened % block_count
    entries = flattened.shape[0]
    offset = (position - owner_device // stride) % SPAN
    alike = offset[:, None] == offset[None, :]
    earlier = jnp.arange(entries)[None, :] < jnp.arange(entries)[:, None]
    ranking = jnp.sum(jnp.where(alike & earlier, 1, 0), axis=1).astype(jnp.int32)
    slots = offset * capacity + ranking
    columns = jnp.arange(SPAN * LANES, dtype=jnp.int32)
    matches = (offset * LANES + ranking)[None, :] == columns[:, None]
    tables = jnp.sum(jnp.where(matches, within[None, :], 0), axis=1)
    return slots, tables.astype(jnp.int32).reshape(SPAN, 1, LANES)


def place_kernel(local_ref, features_ref, placed_ref, normed_ref):
    groups, _, size = local_ref.shape
    lane = lax.broadcasted_iota(jnp.int32, (size, LANES), 1).astype(jnp.float32)
    for i in range(groups):
        rows = pl.ds(i * size, size)
        takes = jnp.broadcast_to(local_ref[i].astype(jnp.float32), (LANES, size)).T
        one_hot = jnp.concatenate(
            [jnp.where(takes == lane + k, 1.0, 0.0) for k in range(0, size, LANES)], axis=1
        ).astype(jnp.bfloat16)
        placed = jnp.dot(one_hot, features_ref[rows, :], preferred_element_type=jnp.float32)
        placed_ref[rows, :] = placed.astype(jnp.bfloat16)
        normed_ref[rows, :] = layer_norm(placed).astype(jnp.bfloat16)


def exchange_kernel(
    capacity, stride, blocks_ref, tables_ref, arrived_ref,
    wanted, wanted_s, outbox, t_send, t_recv, d_send, d_recv, local_sem,
):
    me = lax.axis_index("elec")
    group = lax.axis_index("groups")
    peers = lax.axis_size("elec")
    cluster = blocks_ref.shape[1]

    def toward(step):
        return (group, lax.rem(me + step * stride + peers, peers))

    barrier = pltpu.get_barrier_semaphore()
    for step in range(1, SPAN):
        pl.semaphore_signal(barrier, inc=1, device_id=toward(step), device_id_type=MESH)
    pl.semaphore_wait(barrier, SPAN - 1)

    order = sorted(range(1, SPAN), key=lambda s: abs(s - SPAN // 2))
    asks = {}
    for step in order:
        asks[step] = pltpu.make_async_remote_copy(
            src_ref=tables_ref.at[step], dst_ref=wanted.at[step],
            send_sem=t_send.at[step], recv_sem=t_recv.at[step],
            device_id=toward(-step), device_id_type=MESH,
        )
        asks[step].start()

    def gather(step, source):
        copy = pltpu.make_async_copy(source, wanted_s.at[step], local_sem.at[step])
        copy.start()
        copy.wait()

        def one(k, carry):
            start = pl.multiple_of(k * cluster, cluster)
            outbox[step, pl.ds(start, cluster), :] = blocks_ref[wanted_s[step, 0, k]]
            return carry

        lax.fori_loop(0, capacity, one, 0)

    sends = []
    for step in order:
        asks[step].wait_recv()
        gather(step, wanted.at[step])
        send = pltpu.make_async_remote_copy(
            src_ref=outbox.at[step], dst_ref=arrived_ref.at[step],
            send_sem=d_send.at[step], recv_sem=d_recv.at[step],
            device_id=toward(step), device_id_type=MESH,
        )
        send.start()
        sends.append(send)
    gather(0, tables_ref.at[0])
    own = pltpu.make_async_copy(outbox.at[0], arrived_ref.at[0], local_sem.at[SPAN])
    own.start()
    for step in order:
        asks[step].wait_send()
    own.wait()
    for send in sends:
        send.wait()


def attend_kernel(
    slots_ref, placed_ref, normed_ref, arrived_ref, wq_ref, wk_ref, wv_ref, wo_ref, wm_ref,
    out_ref, queries, attended,
):
    cluster, width = arrived_ref.shape[1:]
    rows = placed_ref.shape[0]
    blocks = rows // cluster
    pair_count = slots_ref.shape[0] // (blocks * pl.num_programs(0))
    head_width = width // HEADS
    half = LANES // 2
    per = half // head_width
    first = pl.program_id(0) * blocks
    f32, bf16 = jnp.float32, jnp.bfloat16
    lane = lax.broadcasted_iota(jnp.int32, (cluster, LANES), 1)
    low = lane < half
    low_keys = lax.broadcasted_iota(jnp.int32, ((pair_count + 1) * cluster, LANES), 1) < half
    chosen = [jnp.where(lane // head_width == c, 1.0, 0.0).astype(bf16) for c in range(2 * per)]
    own_head = lane % half // head_width
    scale = math.log2(math.e) / head_width**0.5
    queries[...] = (
        jnp.dot(normed_ref[...], wq_ref[...], preferred_element_type=f32) * scale
    ).astype(bf16)

    def one(j, carry):
        start = pl.multiple_of(j * cluster, cluster)
        base = (first + j) * pair_count
        listed = [arrived_ref[slots_ref[base + p]] for p in range(pair_count)]
        key_rows = jnp.concatenate([normed_ref[pl.ds(start, cluster), :]] + listed, axis=0)
        keys = jnp.dot(key_rows, wk_ref[...], preferred_element_type=f32).astype(bf16)
        values = jnp.dot(key_rows, wv_ref[...], preferred_element_type=f32)
        for band in range(0, width, LANES):
            query = queries[pl.ds(start, cluster), band : band + LANES]
            band_keys = keys[:, band : band + LANES]
            band_values = values[:, band : band + LANES]
            folded = []
            for side in range(2):
                stacked = jnp.concatenate(
                    [query * chosen[side * per + c] for c in range(per)], axis=0
                )
                scores = lax.dot_general(
                    stacked, band_keys, (((1,), (1,)), ((), ())), preferred_element_type=f32
                )
                weights = jnp.exp2(scores - jnp.max(scores, axis=1, keepdims=True)).astype(bf16)
                with_ones = (
                    jnp.where(low_keys, band_values, 1.0)
                    if side == 0
                    else jnp.where(low_keys, 1.0, band_values)
                ).astype(bf16)
                result = jnp.dot(weights, with_ones, preferred_element_type=f32)
                kept = result[(per - 1) * cluster :]
                for c in range(per - 1):
                    kept = jnp.where(own_head == c, result[c * cluster : (c + 1) * cluster], kept)
                folded.append(kept)
            numerator = jnp.where(low, folded[0], folded[1])
            denominator = pltpu.roll(jnp.where(low, folded[1], folded[0]), half, 1)
            attended[pl.ds(start, cluster), band : band + LANES] = (
                numerator / denominator
            ).astype(bf16)
        return carry

    lax.fori_loop(0, blocks, one, 0, unroll=True)
    projected = jnp.dot(attended[...], wo_ref[...], preferred_element_type=f32)
    middle = (placed_ref[...].astype(f32) + projected).astype(bf16).astype(f32)
    second = layer_norm(middle).astype(bf16)
    mixed = middle + jnp.tanh(jnp.dot(second, wm_ref[...], preferred_element_type=f32))
    out_ref[...] = mixed.astype(bf16)


def body(features, assignment, pairs, w_query, w_key, w_value, w_out, w_mix):
    rows_dev, width = features.shape
    block_count, pair_count = pairs.shape
    cluster = rows_dev // block_count
    capacity = (block_count * pair_count + SPAN - 1) // SPAN + 1
    stride = lax.axis_size("elec") // SPAN
    device_index = lax.axis_index("elec")
    position = device_index // stride
    group_rows = SPAN * cluster
    groups = rows_dev // group_rows
    bf16 = jnp.bfloat16

    local = (assignment - device_index * rows_dev).reshape(groups, 1, group_rows)
    local = local - group_rows * jnp.arange(groups, dtype=jnp.int32)[:, None, None]
    batch = math.gcd(groups, 2)
    tile = pl.BlockSpec((batch * group_rows, width), lambda i: (i, 0))
    placed, normed = pl.pallas_call(
        place_kernel,
        grid=(groups // batch,),
        in_specs=[pl.BlockSpec((batch, 1, group_rows), lambda i: (i, 0, 0)), tile],
        out_specs=[tile, tile],
        out_shape=[jax.ShapeDtypeStruct((rows_dev, width), bf16)] * 2,
    )(local, features)

    slots, tables = slot_table(pairs, block_count, capacity, position, stride)
    arrived = pl.pallas_call(
        functools.partial(exchange_kernel, capacity, stride),
        in_specs=[pl.BlockSpec(memory_space=pltpu.VMEM)] * 2,
        out_specs=pl.BlockSpec(memory_space=pl.ANY),
        out_shape=jax.ShapeDtypeStruct((SPAN, capacity * cluster, width), bf16),
        scratch_shapes=[
            pltpu.VMEM((SPAN, 1, LANES), jnp.int32),
            pltpu.SMEM((SPAN, 1, LANES), jnp.int32),
            pltpu.VMEM((SPAN, capacity * cluster, width), bf16),
            pltpu.SemaphoreType.DMA((SPAN,)),
            pltpu.SemaphoreType.DMA((SPAN,)),
            pltpu.SemaphoreType.DMA((SPAN,)),
            pltpu.SemaphoreType.DMA((SPAN,)),
            pltpu.SemaphoreType.DMA((SPAN + 1,)),
        ],
        compiler_params=pltpu.CompilerParams(
            collective_id=0, has_side_effects=True, vmem_limit_bytes=32 * 2**20
        ),
    )(normed.reshape(block_count, cluster, width), tables)
    arrived = arrived.reshape(SPAN * capacity, cluster, width)

    tile = pl.BlockSpec((group_rows, width), lambda i, s: (i, 0))
    weight = pl.BlockSpec((width, width), lambda i, s: (0, 0))
    return pl.pallas_call(
        attend_kernel,
        grid_spec=pltpu.PrefetchScalarGridSpec(
            num_scalar_prefetch=1,
            grid=(groups,),
            in_specs=[
                tile,
                tile,
                pl.BlockSpec(arrived.shape, lambda i, s: (0, 0, 0)),
            ]
            + [weight] * 5,
            out_specs=tile,
            scratch_shapes=[pltpu.VMEM((group_rows, width), bf16)] * 2,
        ),
        out_shape=jax.ShapeDtypeStruct((rows_dev, width), bf16),
        compiler_params=pltpu.CompilerParams(vmem_limit_bytes=48 * 2**20),
    )(slots, placed, normed, arrived, w_query, w_key, w_value, w_out, w_mix)


def solution(mesh):
    placed = (
        P(("groups", "elec"), None),
        P(("groups", "elec")),
        P(("groups", "elec"), None),
        P(),
        P(),
        P(),
        P(),
        P(),
    )
    return jax.shard_map(
        body, mesh=mesh, in_specs=placed, out_specs=P(("groups", "elec"), None), check_vma=False
    )
```
